32 devices in a mesh: dp: 4 (over y, core), ctx: 4 (over z), tp: 2 (over x).
Axes of the slice: x: 2, y: 2, z: 4, core: 2. Of those that a mesh axis runs over, the one named last changes fastest.
Arguments:
- tokens: bfloat16 [4, 1024, 8192], P('dp', 'ctx', 'tp'), may hold values from -6 to 6
- queries: bfloat16 [4, 1024, 8192], P('dp', 'ctx', 'tp'), may hold values from -180 to 180
- k_weight: bfloat16 [8192, 512], P('dp', 'tp'), may hold values from -0.0625 to 0.0625
- v_weight: bfloat16 [8192, 512], P('dp', 'tp'), may hold values from -0.0625 to 0.0625
- doc_blocks: int32 [4, 8], P('dp', 'ctx'), may hold values from 0 to 3, never falling along the last dimension, each value on 1 to 4 neighbouring positions
Outputs:
- context: bfloat16 [4, 1024, 8192], P('dp', 'ctx', 'tp')
The draws below stay inside these ranges and needn't reach their ends.
Inputs may be any that keep to these rules, and one draw needn't show every extreme that they name: `doc_blocks`: along each sequence the document numbers never fall; each document covers 1 to 4 whole blocks, one exactly 4.
All inputs are finite; a program needn't handle non-finite values.
Results may differ from the reference program's by a relative error of at most 0.012.
The reference program's roundings to bfloat16 on the way count: a program that leaves them out, or rounds other values in their place, can miss the bound.
Values may be sent and summed in bfloat16 or wider, within the bound.
A program may use at most 192 MiB of HBM per device.

```python
import math
import jax
import jax.numpy as jnp
import numpy as np
from jax import lax

D = 8192
QH = 64
KVH = 4
HD = 128
BLOCK = 128
DOCS = 4
TOK_DEV = 256
SEQS = 4
LEN = 1024
NBLK = 8
N_CTX = 4


def draw_queries(key, part):
    key_base = jax.random.fold_in(key, 11)
    drawn = jnp.clip(jax.random.normal(key_base, (SEQS, LEN, QH * HD), jnp.float32), -4.0, 4.0)
    return drawn.astype(jnp.bfloat16)


def steps_of(rng, extent, pieces, low, high):
    level = 1.0
    for position, blocks in pieces:
        steps = jax.random.uniform(jax.random.fold_in(jax.random.fold_in(rng, 6), position), (blocks,), jnp.float32, low / len(pieces), high / len(pieces))
        level = level * jnp.repeat(jnp.exp(steps), extent[position] // blocks).reshape((-1,) + (1,) * (len(extent) - 1 - position))
    return level


def profile(amount, total, limit, skew):
    loads = [(1 << 20) // math.isqrt(standing ** skew) + 1 for standing in range(2, amount + 1)]
    spare, counts = total - limit - (amount - 1), [1] * (amount - 1)
    while spare > 0:
        candidates = [i for i in range(amount - 1) if counts[i] < limit]
        whole, left = sum([loads[i] for i in candidates]), spare
        for i in candidates:
            extra = min(limit - counts[i], max(1, left * loads[i] // whole), spare)
            counts[i] = counts[i] + extra
            spare = spare - extra
    return np.array([limit] + counts)


def ragged_sizes(key, count, total, most, lean):
    if count == 2:
        one = jax.random.randint(key, (), max(1, total - most), min(most, total - 1) + 1)
        return jnp.stack([one, total - one])
    tallies = jnp.asarray(profile(count, total, most, lean), jnp.int32)
    pairs = (count - 1) // 2
    donor, receiver = tallies[1:1 + 2 * pairs:2], tallies[2:2 + 2 * pairs:2]
    margin = jnp.minimum(donor - 1, most - receiver)
    moved = jax.random.randint(jax.random.fold_in(key, 1), (pairs,), 0, 1 << 20) % (margin + 1)
    tallies = tallies.at[1:1 + 2 * pairs:2].set(donor - moved).at[2:2 + 2 * pairs:2].set(receiver + moved)
    return tallies[jax.random.permutation(jax.random.fold_in(key, 2), count)]


def centred(own_key, extent, deviation, most, split=(), kind=jnp.bfloat16):
    level = steps_of(own_key, extent, split, -0.22, 0.18) if split else 1.0
    result = jax.random.normal(own_key, extent, jnp.float32) * deviation * level
    return jnp.minimum(jnp.maximum(result, -most), most).astype(kind)


def setup_inputs(seed: int = 0) -> dict:
    keys = jax.random.split(jax.random.key(seed), 6)
    return {
        "tokens": centred(keys[0], (SEQS, LEN, D), 1.0, 6.0, ((0, 4), (1, 4), (2, 2))),
        "queries": draw_queries(jax.random.fold_in(keys[5], 71), 0),
        "k_weight": centred(keys[2], (D, KVH * HD), D ** -0.5, 0.0625, ((0, 4), (1, 2))),
        "v_weight": centred(keys[3], (D, KVH * HD), D ** -0.5, 0.0625, ((0, 4), (1, 2))),
        "doc_blocks": jax.vmap(lambda own: jnp.searchsorted(jnp.cumsum(ragged_sizes(own, DOCS, NBLK, NBLK // 2, 0)), jnp.arange(NBLK), side="right"))(jax.random.split(keys[4], SEQS)).reshape((SEQS, NBLK)).astype(jnp.int32),
    }


ROPE_BASE = 500000.0
YARN_FACTOR = 16.0
PRETRAIN_CONTEXT = 8192.0
BETA_FAST = 32.0
BETA_SLOW = 1.0
ATTN_FACTOR = (1.0 + 0.1 * math.log(16.0)) ** 2

def yarn_tables(positions):
    counter = jnp.arange(HD // 2, dtype=jnp.float32)
    base_freq = ROPE_BASE ** (-2.0 * counter / HD)
    wave_ratio = PRETRAIN_CONTEXT * base_freq / (2.0 * math.pi)
    ramp_value = jnp.clip((wave_ratio - BETA_SLOW) / (BETA_FAST - BETA_SLOW), 0.0, 1.0)
    frequency = ramp_value * base_freq + (1.0 - ramp_value) * base_freq / YARN_FACTOR
    angles = positions.astype(jnp.float32)[:, None] * frequency[None, :]
    cosine = jnp.cos(angles)
    sine_table = jnp.sin(angles)
    return (jnp.concatenate([cosine, cosine], axis=-1), jnp.concatenate([sine_table, sine_table], axis=-1))

def rotate(vectors, cosine, sine_table):
    half_width = vectors.shape[-1] // 2
    lower_half = vectors[..., :half_width]
    upper_half = vectors[..., half_width:]
    turned = jnp.concatenate([-upper_half, lower_half], axis=-1)
    return vectors * cosine[:, None, :] + turned * sine_table[:, None, :]

def reference(tokens, queries, k_weight, v_weight, doc_blocks):
    group_size = QH // KVH

    def one_sequence(packed):
        seq_tokens, seq_queries, seq_docs = packed
        key_proj = jnp.dot(seq_tokens, k_weight, preferred_element_type=jnp.float32)
        value_proj = jnp.dot(seq_tokens, v_weight, preferred_element_type=jnp.float32)
        positions = jnp.arange(LEN, dtype=jnp.int32)
        cosine, sine_table = yarn_tables(positions)
        key_rows = rotate(key_proj.reshape(LEN, KVH, HD), cosine, sine_table).astype(jnp.bfloat16)
        value_rows = value_proj.reshape(LEN, KVH, HD).astype(jnp.bfloat16)
        query_rot = (rotate(seq_queries.astype(jnp.float32).reshape(LEN, QH, HD), cosine, sine_table) * (ATTN_FACTOR / math.sqrt(HD))).astype(jnp.bfloat16)
        token_docs = jnp.repeat(seq_docs, BLOCK)
        key_float = key_rows.astype(jnp.float32)
        value_float = value_rows.astype(jnp.float32)

        def one_block(block_id):
            begin_row = (block_id * TOK_DEV).astype(jnp.int32)
            query_block = lax.dynamic_slice_in_dim(query_rot, begin_row, TOK_DEV, 0).astype(jnp.float32)
            query_block = query_block.reshape(TOK_DEV, KVH, group_size, HD)
            query_pos = begin_row + jnp.arange(TOK_DEV, dtype=jnp.int32)
            query_docs = lax.dynamic_slice_in_dim(token_docs, begin_row, TOK_DEV, 0)
            visible = (positions[None, :] <= query_pos[:, None]) & (token_docs[None, :] == query_docs[:, None])
            scores = jnp.einsum('qkgd,nkd->kgqn', query_block, key_float)
            scores = jnp.where(visible, scores, -jnp.inf)
            row_top = lax.optimization_barrier(jnp.max(scores, axis=-1, keepdims=True))
            weights = jnp.exp(scores - row_top)
            denominator = lax.optimization_barrier(jnp.sum(weights, axis=-1))
            mixed_values = jnp.einsum('kgqn,nkd->kgqd', weights.astype(jnp.bfloat16).astype(jnp.float32), value_float)
            attended = mixed_values / denominator[..., None]
            return attended.transpose(2, 0, 1, 3).reshape(TOK_DEV, QH * HD).astype(jnp.bfloat16)
        blocks = lax.map(one_block, jnp.arange(N_CTX, dtype=jnp.int32))
        return blocks.reshape(LEN, QH * HD)
    return lax.map(one_sequence, (tokens, queries, doc_blocks))
```

```python
import functools
import math

import jax
import jax.numpy as jnp
import numpy as np
from jax import lax
from jax.experimental import pallas as pl
from jax.experimental.pallas import tpu as pltpu
from jax.sharding import PartitionSpec as P

HD = 128
BLOCK = 128
STEPS = 4
HEADS_AT_ONCE = 4

ROPE_BASE = 500000.0
YARN_FACTOR = 16.0
PRETRAIN_CONTEXT = 8192.0
BETA_FAST = 32.0
BETA_SLOW = 1.0
ATTN_FACTOR = (1.0 + 0.1 * math.log(16.0)) ** 2
MASKED_SCORE = -1e30
MESH = pl.DeviceIdType.MESH


def yarn_frequency():
    counter = np.arange(HD // 2, dtype=np.float64)
    base_freq = ROPE_BASE ** (-2.0 * counter / HD)
    wave_ratio = PRETRAIN_CONTEXT * base_freq / (2.0 * math.pi)
    ramp = np.clip((wave_ratio - BETA_SLOW) / (BETA_FAST - BETA_SLOW), 0.0, 1.0)
    frequency = ramp * base_freq + (1.0 - ramp) * base_freq / YARN_FACTOR
    return np.concatenate([frequency, frequency]).astype(np.float32)


def kernel(
    sizes,
    tok_hbm, q_hbm, kw_hbm, vw_hbm, freq_ref, docs_ref,
    out_ref,
    tok, qraw, qrot, wk, wv, acc, kv, docs, cos_ref, sin_ref,
    loc_sem, y_send, y_recv, s_send, s_recv, f_send, f_recv, t_send, t_recv,
    kv_send, kv_recv, d_send, d_recv,
):
    dp, n_ctx, tp = sizes
    groups = dp // 2
    pieces = dp // tp
    rows = q_hbm.shape[0]
    deep = kw_hbm.shape[0]
    part = deep // STEPS
    kvw = kw_hbm.shape[1]
    kv_heads = kvw // HD
    heads = q_hbm.shape[1] // HD
    back = docs.shape[0] - 1
    nb = rows // BLOCK
    span = nb * n_ctx // 2
    me_dp = lax.axis_index("dp")
    me_ctx = lax.axis_index("ctx")
    me_tp = lax.axis_index("tp")
    group = me_dp // 2
    core = me_dp % 2
    sib = group * 2 + (1 - core)

    def remote(src, dst, send, recv, where):
        return pltpu.make_async_remote_copy(
            src_ref=src, dst_ref=dst, send_sem=send, recv_sem=recv,
            device_id=where, device_id_type=MESH,
        )

    locals_ = [
        pltpu.make_async_copy(q_hbm, qraw, loc_sem.at[0]),
        pltpu.make_async_copy(kw_hbm, wk.at[me_dp], loc_sem.at[1]),
        pltpu.make_async_copy(vw_hbm, wv.at[me_dp], loc_sem.at[2]),
    ]
    for j in range(pieces):
        locals_.append(
            pltpu.make_async_copy(
                tok_hbm.at[:, pl.ds(j * deep, deep)],
                tok.at[me_tp * pieces + j],
                loc_sem.at[3 + j],
            )
        )
    for one in locals_:
        one.start()

    barrier = pltpu.get_barrier_semaphore()
    fixed = 0
    for r in range(1, groups):
        other = lax.rem(group + r, groups) * 2 + core
        pl.semaphore_signal(barrier, inc=1, device_id={"dp": other}, device_id_type=MESH)
        fixed += 1
    pl.semaphore_signal(barrier, inc=1, device_id={"dp": sib}, device_id_type=MESH)
    fixed += 1
    for r in range(1, tp):
        pl.semaphore_signal(
            barrier, inc=1, device_id={"tp": lax.rem(me_tp + r, tp)}, device_id_type=MESH
        )
        fixed += 1
    for d in range(1, back + 1):
        @pl.when(me_ctx + d < n_ctx)
        def _():
            pl.semaphore_signal(barrier, inc=1, device_id={"ctx": me_ctx + d}, device_id_type=MESH)

        @pl.when(me_ctx - d >= 0)
        def _():
            pl.semaphore_signal(barrier, inc=1, device_id={"ctx": me_ctx - d}, device_id_type=MESH)
    peers = fixed
    for d in range(1, back + 1):
        peers = peers + jnp.where(me_ctx + d < n_ctx, 1, 0) + jnp.where(me_ctx - d >= 0, 1, 0)
    pl.semaphore_wait(barrier, peers)

    started = []
    y_in, s_in, t_in = {}, {}, {}
    for i in range(STEPS):
        cut = pl.ds(i * part, part)
        for r in range(1, groups):
            to = lax.rem(group + r, groups) * 2 + core
            source = lax.rem(group + groups - r, groups) * 2 + core
            for w, (hbm, buf) in enumerate(((kw_hbm, wk), (vw_hbm, wv))):
                copy = remote(
                    hbm.at[cut], buf.at[me_dp, cut],
                    y_send.at[r - 1, i, w], y_recv.at[r - 1, i, w], {"dp": to},
                )
                copy.start()
                started.append(copy)
                y_in[r, i, w] = remote(
                    hbm.at[cut], buf.at[source, cut],
                    y_send.at[r - 1, i, w], y_recv.at[r - 1, i, w], {"dp": to},
                )
        for r in range(1, tp):
            to = lax.rem(me_tp + r, tp)
            source = lax.rem(me_tp + tp - r, tp)
            for j in range(pieces):
                copy = remote(
                    tok_hbm.at[:, pl.ds(j * deep + i * part, part)],
                    tok.at[me_tp * pieces + j, :, cut],
                    t_send.at[r - 1, i, j], t_recv.at[r - 1, i, j], {"tp": to},
                )
                copy.start()
                started.append(copy)
                t_in[r, i, j] = remote(
                    tok_hbm.at[:, pl.ds(j * deep + i * part, part)],
                    tok.at[source * pieces + j, :, cut],
                    t_send.at[r - 1, i, j], t_recv.at[r - 1, i, j], {"tp": to},
                )
        if i == 0:
            for w, (hbm, buf) in enumerate(((kw_hbm, wk), (vw_hbm, wv))):
                copy = remote(
                    hbm, buf.at[me_dp], s_send.at[w], s_recv.at[w], {"dp": sib}
                )
                copy.start()
                started.append(copy)
                s_in[w] = remote(
                    hbm, buf.at[sib], s_send.at[w], s_recv.at[w], {"dp": sib}
                )

    def doc_copy(d):
        return remote(
            docs_ref, docs.at[back - d], d_send.at[d - 1], d_recv.at[d - 1], {"ctx": me_ctx + d}
        )

    def doc_in(d):
        return remote(
            docs_ref, docs.at[back - d], d_send.at[d - 1], d_recv.at[d - 1], {"ctx": me_ctx - d}
        )

    for d in range(1, back + 1):
        @pl.when(me_ctx + d < n_ctx)
        def _():
            doc_copy(d).start()

        @pl.when(me_ctx - d < 0)
        def _():
            docs[back - d] = jnp.full(docs.shape[1:], -1, jnp.int32)
            kv[back - d] = jnp.zeros(kv.shape[1:], kv.dtype)
    docs[back] = docs_ref[...]

    position = me_ctx * rows + lax.broadcasted_iota(jnp.int32, (rows, HD), 0)
    angle = position.astype(jnp.float32) * freq_ref[...]
    upper = lax.broadcasted_iota(jnp.int32, (rows, HD), 1) >= HD // 2
    cos_ref[...] = jnp.cos(angle)
    sine = jnp.sin(angle)
    sin_ref[...] = jnp.where(upper, sine, -sine)
    for one in locals_:
        one.wait()
    scale = ATTN_FACTOR / math.sqrt(HD)

    @pl.loop(0, heads)
    def _(h):
        u = qraw[:, pl.ds(pl.multiple_of(h * HD, HD), HD)].astype(jnp.float32)
        turned = u * cos_ref[...] + pltpu.roll(u, HD // 2, 1) * sin_ref[...]
        qrot[h] = (turned * scale).astype(jnp.bfloat16)

    acc[...] = jnp.zeros_like(acc)
    for w in range(2):
        s_in[w].wait_recv()

    for i in range(STEPS):
        cut = pl.ds(i * part, part)
        forwarded = []
        for r in range(1, groups):
            source = lax.rem(group + groups - r, groups) * 2 + core
            sib_source = lax.rem(group + groups - r, groups) * 2 + (1 - core)
            for w, buf in enumerate((wk, wv)):
                y_in[r, i, w].wait_recv()
                copy = remote(
                    buf.at[source, cut], buf.at[source, cut],
                    f_send.at[r - 1, i, w], f_recv.at[r - 1, i, w], {"dp": sib},
                )
                copy.start()
                started.append(copy)
                forwarded.append(
                    remote(
                        buf.at[sib_source, cut], buf.at[sib_source, cut],
                        f_send.at[r - 1, i, w], f_recv.at[r - 1, i, w], {"dp": sib},
                    )
                )
        for r in range(1, tp):
            for j in range(pieces):
                t_in[r, i, j].wait_recv()
        for copy in forwarded:
            copy.wait_recv()

        @pl.loop(0, dp)
        def _(p):
            x = tok[p, :, cut]
            acc[:, :kvw] += jnp.dot(x, wk[p, cut, :], preferred_element_type=jnp.float32)
            acc[:, kvw:] += jnp.dot(x, wv[p, cut, :], preferred_element_type=jnp.float32)

    for g in range(kv_heads):
        u = acc[:, g * HD:(g + 1) * HD]
        turned = u * cos_ref[...] + pltpu.roll(u, HD // 2, 1) * sin_ref[...]
        kv[back, g, :, :HD] = turned.astype(jnp.bfloat16)
        kv[back, g, :, HD:] = acc[:, kvw + g * HD:kvw + (g + 1) * HD].astype(jnp.bfloat16)

        for d in range(1, back + 1):
            @pl.when(me_ctx + d < n_ctx)
            def _():
                kv_copy(kv, kv_send, kv_recv, remote, back, span, nb, rows, g, d, me_ctx + d).start()

    for d in range(1, back + 1):
        @pl.when(me_ctx - d >= 0)
        def _():
            doc_in(d).wait_recv()

    wide = span * BLOCK
    keep = []
    for b in range(nb):
        first = back * nb + b + 1 - span
        mine = docs[back, 0:1, b * BLOCK:(b + 1) * BLOCK]
        key_docs = jnp.concatenate(
            [
                docs[(first + k) // nb, 0:1, ((first + k) % nb) * BLOCK:((first + k) % nb + 1) * BLOCK] - mine
                for k in range(span)
            ],
            axis=1,
        )
        column = lax.broadcasted_iota(jnp.int32, (BLOCK, wide), 1) - (span - 1) * BLOCK
        row = lax.broadcasted_iota(jnp.int32, (BLOCK, wide), 0)
        keep.append((column <= row) & (key_docs == 0))

    group_heads = heads // kv_heads
    for g in range(kv_heads):
        for d in range(1, back + 1):
            @pl.when(me_ctx - d >= 0)
            def _():
                kv_copy(kv, kv_send, kv_recv, remote, back, span, nb, rows, g, d, me_ctx - d).wait_recv()
        for b in range(nb):
            first = back * nb + b + 1 - span
            window = jnp.concatenate(
                [
                    kv[(first + k) // nb, g, ((first + k) % nb) * BLOCK:((first + k) % nb + 1) * BLOCK, :]
                    for k in range(span)
                ],
                axis=0,
            )
            keys, values = window[:, :HD], window[:, HD:]
            mask = keep[b]

            @pl.loop(0, group_heads // HEADS_AT_ONCE)
            def _(t):
                h0 = g * group_heads + t * HEADS_AT_ONCE
                q = qrot[pl.ds(h0, HEADS_AT_ONCE), b * BLOCK:(b + 1) * BLOCK, :]
                s = lax.dot_general(
                    q.reshape(HEADS_AT_ONCE * BLOCK, HD), keys,
                    (((1,), (1,)), ((), ())), preferred_element_type=jnp.float32,
                ).reshape(HEADS_AT_ONCE, BLOCK, wide)
                s = jnp.where(mask[None], s, MASKED_SCORE)
                top = jnp.max(s, axis=-1, keepdims=True)
                e = jnp.exp(s - top)
                total = jnp.sum(e, axis=-1, keepdims=True)
                mixed = jnp.dot(
                    e.astype(jnp.bfloat16).reshape(HEADS_AT_ONCE * BLOCK, wide), values,
                    preferred_element_type=jnp.float32,
                ).reshape(HEADS_AT_ONCE, BLOCK, HD)
                mixed = (mixed / total).astype(jnp.bfloat16)
                for k in range(HEADS_AT_ONCE):
                    out_ref[b * BLOCK:(b + 1) * BLOCK, pl.ds(pl.multiple_of((h0 + k) * HD, HD), HD)] = mixed[k]

    for copy in started:
        copy.wait_send()
    for d in range(1, back + 1):
        @pl.when(me_ctx + d < n_ctx)
        def _():
            doc_copy(d).wait_send()
            for g in range(kv_heads):
                kv_copy(kv, kv_send, kv_recv, remote, back, span, nb, rows, g, d, me_ctx + d).wait_send()


def kv_copy(kv, send, recv, remote, back, span, nb, rows, g, d, other):
    skip = max(0, d * nb + 1 - span) * BLOCK
    cut = pl.ds(skip, rows - skip)
    return remote(
        kv.at[back, g, cut], kv.at[back - d, g, cut],
        send.at[d - 1, g], recv.at[d - 1, g], {"ctx": other},
    )


def solution(mesh):
    dp, n_ctx, tp = mesh.shape["dp"], mesh.shape["ctx"], mesh.shape["tp"]

    def body(tokens, queries, k_weight, v_weight, doc_blocks):
        rows, width = tokens.shape[1], tokens.shape[2]
        deep, kvw = k_weight.shape
        heads = queries.shape[2] // HD
        nb = rows // BLOCK
        span = nb * n_ctx // 2
        back = -(-(span - 1) // nb)
        groups, pieces = dp // 2, dp // tp
        docs = jnp.broadcast_to(jnp.repeat(doc_blocks[0], BLOCK)[None, :], (8, rows))
        frequency = jnp.asarray(yarn_frequency()).reshape(1, HD)
        dma = pltpu.SemaphoreType.DMA
        anywhere = pl.BlockSpec(memory_space=pl.ANY)
        vmem = pl.BlockSpec(memory_space=pltpu.VMEM)
        out = pl.pallas_call(
            functools.partial(kernel, (dp, n_ctx, tp)),
            out_shape=jax.ShapeDtypeStruct((rows, heads * HD), jnp.bfloat16),
            in_specs=[anywhere] * 4 + [vmem] * 2,
            out_specs=vmem,
            scratch_shapes=[
                pltpu.VMEM((dp, rows, deep), jnp.bfloat16),
                pltpu.VMEM((rows, heads * HD), jnp.bfloat16),
                pltpu.VMEM((heads, rows, HD), jnp.bfloat16),
                pltpu.VMEM((dp, deep, kvw), jnp.bfloat16),
                pltpu.VMEM((dp, deep, kvw), jnp.bfloat16),
                pltpu.VMEM((rows, 2 * kvw), jnp.float32),
                pltpu.VMEM((back + 1, kvw // HD, rows, 2 * HD), jnp.bfloat16),
                pltpu.VMEM((back + 1, 8, rows), jnp.int32),
                pltpu.VMEM((rows, HD), jnp.float32),
                pltpu.VMEM((rows, HD), jnp.float32),
                dma((3 + pieces,)),
                dma((groups - 1, STEPS, 2)), dma((groups - 1, STEPS, 2)),
                dma((2,)), dma((2,)),
                dma((groups - 1, STEPS, 2)), dma((groups - 1, STEPS, 2)),
                dma((tp - 1, STEPS, pieces)), dma((tp - 1, STEPS, pieces)),
                dma((back, kvw // HD)), dma((back, kvw // HD)),
                dma((back,)), dma((back,)),
            ],
            compiler_params=pltpu.CompilerParams(
                collective_id=0, has_side_effects=True, vmem_limit_bytes=48 << 20
            ),
        )(tokens[0], queries[0], k_weight, v_weight, frequency, docs)
        return out[None]

    placed = (
        P("dp", "ctx", "tp"),
        P("dp", "ctx", "tp"),
        P("dp", "tp"),
        P("dp", "tp"),
        P("dp", "ctx"),
    )
    return jax.shard_map(
        body, mesh=mesh, in_specs=placed, out_specs=P("dp", "ctx", "tp"), check_vma=False
    )
```

```python
import functools
import math

import jax
import jax.numpy as jnp
from jax import lax
from jax.experimental import pallas as pl
from jax.experimental.pallas import tpu as pltpu
from jax.sharding import PartitionSpec as P

HD = 128
BLOCK = 128
STEPS = 4
HEADS_AT_ONCE = 8

ROPE_BASE = 500000.0
YARN_FACTOR = 16.0
PRETRAIN_CONTEXT = 8192.0
BETA_FAST = 32.0
BETA_SLOW = 1.0
ATTN_FACTOR = (1.0 + 0.1 * math.log(16.0)) ** 2
MASKED_SCORE = -1e30
MESH = pl.DeviceIdType.MESH


def yarn_frequency(shape):
    counter = lax.broadcasted_iota(jnp.int32, shape, 1) % (HD // 2)
    base_freq = jnp.exp(counter.astype(jnp.float32) * (-2.0 * math.log(ROPE_BASE) / HD))
    wave_ratio = base_freq * (PRETRAIN_CONTEXT / (2.0 * math.pi))
    ramp = jnp.clip((wave_ratio - BETA_SLOW) / (BETA_FAST - BETA_SLOW), 0.0, 1.0)
    return ramp * base_freq + (1.0 - ramp) * base_freq / YARN_FACTOR


def kernel(
    sizes,
    tok_hbm, q_hbm, kw_hbm, vw_hbm, docs_hbm,
    out_ref,
    tok, qraw, qrot, wk, wv, acc, kv, docs, docs_own, cos_ref, sin_ref,
    loc_sem, y_send, y_recv, s_send, s_recv, f_send, f_recv, t_send, t_recv,
    kv_send, kv_recv, d_send, d_recv,
):
    dp, n_ctx, tp = sizes
    groups = dp // 2
    pieces = dp // tp
    rows = q_hbm.shape[0]
    deep = kw_hbm.shape[0]
    part = deep // STEPS
    kvw = kw_hbm.shape[1]
    kv_heads = kvw // HD
    heads = q_hbm.shape[1] // HD
    back = docs.shape[0] - 1
    nb = rows // BLOCK
    span = nb * n_ctx // 2
    me_dp = lax.axis_index("dp")
    me_ctx = lax.axis_index("ctx")
    me_tp = lax.axis_index("tp")
    group = me_dp // 2
    core = me_dp % 2
    sib = group * 2 + (1 - core)

    def remote(src, dst, send, recv, where):
        return pltpu.make_async_remote_copy(
            src_ref=src, dst_ref=dst, send_sem=send, recv_sem=recv,
            device_id=where, device_id_type=MESH,
        )

    locals_ = [
        pltpu.make_async_copy(q_hbm, qraw, loc_sem.at[0]),
        pltpu.make_async_copy(kw_hbm, wk.at[me_dp], loc_sem.at[1]),
        pltpu.make_async_copy(vw_hbm, wv.at[me_dp], loc_sem.at[2]),
    ]
    for j in range(pieces):
        locals_.append(
            pltpu.make_async_copy(
                tok_hbm.at[:, pl.ds(j * deep, deep)],
                tok.at[me_tp * pieces + j],
                loc_sem.at[3 + j],
            )
        )
    docs_in = pltpu.make_async_copy(docs_hbm, docs_own, loc_sem.at[3 + pieces])
    docs_in.start()
    for one in locals_:
        one.start()

    barrier = pltpu.get_barrier_semaphore()
    fixed = 0
    for r in range(1, groups):
        other = lax.rem(group + r, groups) * 2 + core
        pl.semaphore_signal(barrier, inc=1, device_id={"dp": other}, device_id_type=MESH)
        fixed += 1
    pl.semaphore_signal(barrier, inc=1, device_id={"dp": sib}, device_id_type=MESH)
    fixed += 1
    for r in range(1, tp):
        pl.semaphore_signal(
            barrier, inc=1, device_id={"tp": lax.rem(me_tp + r, tp)}, device_id_type=MESH
        )
        fixed += 1
    for d in range(1, back + 1):
        @pl.when(me_ctx + d < n_ctx)
        def _():
            pl.semaphore_signal(barrier, inc=1, device_id={"ctx": me_ctx + d}, device_id_type=MESH)

        @pl.when(me_ctx - d >= 0)
        def _():
            pl.semaphore_signal(barrier, inc=1, device_id={"ctx": me_ctx - d}, device_id_type=MESH)
    peers = fixed
    for d in range(1, back + 1):
        peers = peers + jnp.where(me_ctx + d < n_ctx, 1, 0) + jnp.where(me_ctx - d >= 0, 1, 0)
    pl.semaphore_wait(barrier, peers)

    started = []
    y_in, s_in, t_in = {}, {}, {}
    def start_step(i):
        cut = pl.ds(i * part, part)
        for r in range(1, groups):
            to = lax.rem(group + r, groups) * 2 + core
            source = lax.rem(group + groups - r, groups) * 2 + core
            for w, (hbm, buf) in enumerate(((kw_hbm, wk), (vw_hbm, wv))):
                copy = remote(
                    hbm.at[cut], buf.at[me_dp, cut],
                    y_send.at[r - 1, i, w], y_recv.at[r - 1, i, w], {"dp": to},
                )
                copy.start()
                started.append(copy)
                y_in[r, i, w] = remote(
                    hbm.at[cut], buf.at[source, cut],
                    y_send.at[r - 1, i, w], y_recv.at[r - 1, i, w], {"dp": to},
                )
        for r in range(1, tp):
            to = lax.rem(me_tp + r, tp)
            source = lax.rem(me_tp + tp - r, tp)
            for j in range(pieces):
                copy = remote(
                    tok_hbm.at[:, pl.ds(j * deep + i * part, part)],
                    tok.at[me_tp * pieces + j, :, cut],
                    t_send.at[r - 1, i, j], t_recv.at[r - 1, i, j], {"tp": to},
                )
                copy.start()
                started.append(copy)
                t_in[r, i, j] = remote(
                    tok_hbm.at[:, pl.ds(j * deep + i * part, part)],
                    tok.at[source * pieces + j, :, cut],
                    t_send.at[r - 1, i, j], t_recv.at[r - 1, i, j], {"tp": to},
                )

    start_step(0)
    for w, (hbm, buf) in enumerate(((kw_hbm, wk), (vw_hbm, wv))):
        copy = remote(
            hbm, buf.at[me_dp], s_send.at[w], s_recv.at[w], {"dp": sib}
        )
        copy.start()
        started.append(copy)
        s_in[w] = remote(
            hbm, buf.at[sib], s_send.at[w], s_recv.at[w], {"dp": sib}
        )
    start_step(1)

    def doc_copy(d):
        return remote(
            docs.at[back], docs.at[back - d], d_send.at[d - 1], d_recv.at[d - 1], {"ctx": me_ctx + d}
        )

    def doc_in(d):
        return remote(
            docs.at[back], docs.at[back - d], d_send.at[d - 1], d_recv.at[d - 1], {"ctx": me_ctx - d}
        )

    docs_in.wait()
    lane = lax.broadcasted_iota(jnp.int32, docs.shape[1:], 1)
    spread = jnp.broadcast_to(docs_own[0:1, 0:1], docs.shape[1:])
    for b in range(1, nb):
        spread = jnp.where(lane >= b * BLOCK, docs_own[0:1, b:b + 1], spread)
    docs[back] = spread
    for d in range(1, back + 1):
        @pl.when(me_ctx + d < n_ctx)
        def _():
            doc_copy(d).start()

        @pl.when(me_ctx - d < 0)
        def _():
            docs[back - d] = jnp.full(docs.shape[1:], -1, jnp.int32)
            kv[back - d] = jnp.zeros(kv.shape[1:], kv.dtype)

    position = me_ctx * rows + lax.broadcasted_iota(jnp.int32, (rows, HD), 0)
    angle = position.astype(jnp.float32) * yarn_frequency((1, HD))
    upper = lax.broadcasted_iota(jnp.int32, (rows, HD), 1) >= HD // 2
    cos_ref[...] = jnp.cos(angle)
    sine = jnp.sin(angle)
    sin_ref[...] = jnp.where(upper, sine, -sine)
    for one in locals_:
        one.wait()
    scale = ATTN_FACTOR / math.sqrt(HD)

    @pl.loop(0, heads)
    def _(h):
        u = qraw[:, pl.ds(pl.multiple_of(h * HD, HD), HD)].astype(jnp.float32)
        turned = u * cos_ref[...] + pltpu.roll(u, HD // 2, 1) * sin_ref[...]
        qrot[h] = (turned * scale).astype(jnp.bfloat16)

    acc[...] = jnp.zeros_like(acc)
    for w in range(2):
        s_in[w].wait_recv()

    for i in range(STEPS):
        cut = pl.ds(i * part, part)
        forwarded = []
        for r in range(1, groups):
            source = lax.rem(group + groups - r, groups) * 2 + core
            sib_source = lax.rem(group + groups - r, groups) * 2 + (1 - core)
            for w, buf in enumerate((wk, wv)):
                y_in[r, i, w].wait_recv()
                copy = remote(
                    buf.at[source, cut], buf.at[source, cut],
                    f_send.at[r - 1, i, w], f_recv.at[r - 1, i, w], {"dp": sib},
                )
                copy.start()
                started.append(copy)
                forwarded.append(
                    remote(
                        buf.at[sib_source, cut], buf.at[sib_source, cut],
                        f_send.at[r - 1, i, w], f_recv.at[r - 1, i, w], {"dp": sib},
                    )
                )
        for r in range(1, tp):
            for j in range(pieces):
                t_in[r, i, j].wait_recv()
        for copy in forwarded:
            copy.wait_recv()

        if i + 2 < STEPS:
            start_step(i + 2)

        @pl.loop(0, dp)
        def _(p):
            x = tok[p, :, cut]
            acc[:, :kvw] += jnp.dot(x, wk[p, cut, :], preferred_element_type=jnp.float32)
            acc[:, kvw:] += jnp.dot(x, wv[p, cut, :], preferred_element_type=jnp.float32)

    for g in range(kv_heads):
        u = acc[:, g * HD:(g + 1) * HD]
        turned = u * cos_ref[...] + pltpu.roll(u, HD // 2, 1) * sin_ref[...]
        kv[back, g, :, :HD] = turned.astype(jnp.bfloat16)
        kv[back, g, :, HD:] = acc[:, kvw + g * HD:kvw + (g + 1) * HD].astype(jnp.bfloat16)
    for d in range(1, back + 1):
        for g in range(kv_heads):
            if d > 1:
                @pl.when(me_ctx + d - 1 < n_ctx)
                def _():
                    kv_copy(kv, kv_send, kv_recv, remote, back, span, nb, rows, g, d - 1, me_ctx + d - 1).wait_send()
        for g in range(kv_heads):
            @pl.when(me_ctx + d < n_ctx)
            def _():
                kv_copy(kv, kv_send, kv_recv, remote, back, span, nb, rows, g, d, me_ctx + d).start()

    for d in range(1, back + 1):
        @pl.when(me_ctx - d >= 0)
        def _():
            doc_in(d).wait_recv()

    wide = span * BLOCK
    keep = []
    for b in range(nb):
        first = back * nb + b + 1 - span
        mine = docs[back, 0:1, b * BLOCK:(b + 1) * BLOCK]
        key_docs = jnp.concatenate(
            [
                docs[(first + k) // nb, 0:1, ((first + k) % nb) * BLOCK:((first + k) % nb + 1) * BLOCK] - mine
                for k in range(span)
            ],
            axis=1,
        )
        column = lax.broadcasted_iota(jnp.int32, (BLOCK, wide), 1) - (span - 1) * BLOCK
        row = lax.broadcasted_iota(jnp.int32, (BLOCK, wide), 0)
        keep.append((column <= row) & (key_docs == 0))

    group_heads = heads // kv_heads
    reached = [0] * kv_heads
    for b in reversed(range(nb)):
        first = back * nb + b + 1 - span
        for g in range(kv_heads):
            for d in range(reached[g] + 1, back - first // nb + 1):
                @pl.when(me_ctx - d >= 0)
                def _():
                    kv_copy(kv, kv_send, kv_recv, remote, back, span, nb, rows, g, d, me_ctx - d).wait_recv()
            reached[g] = max(reached[g], back - first // nb)
            window = jnp.concatenate(
                [
                    kv[(first + k) // nb, g, ((first + k) % nb) * BLOCK:((first + k) % nb + 1) * BLOCK, :]
                    for k in range(span)
                ],
                axis=0,
            )
            keys, values = window[:, :HD], window[:, HD:]
            mask = keep[b]

            @pl.loop(0, group_heads // HEADS_AT_ONCE)
            def _(t):
                h0 = g * group_heads + t * HEADS_AT_ONCE
                q = qrot[pl.ds(h0, HEADS_AT_ONCE), b * BLOCK:(b + 1) * BLOCK, :]
                s = lax.dot_general(
                    q.reshape(HEADS_AT_ONCE * BLOCK, HD), keys,
                    (((1,), (1,)), ((), ())), preferred_element_type=jnp.float32,
                ).reshape(HEADS_AT_ONCE, BLOCK, wide)
                s = jnp.where(mask[None], s, MASKED_SCORE)
                top = jnp.max(s, axis=-1, keepdims=True)
                e = jnp.exp(s - top)
                total = jnp.sum(e, axis=-1, keepdims=True)
                mixed = jnp.dot(
                    e.astype(jnp.bfloat16).reshape(HEADS_AT_ONCE * BLOCK, wide), values,
                    preferred_element_type=jnp.float32,
                ).reshape(HEADS_AT_ONCE, BLOCK, HD)
                mixed = (mixed * (1.0 / total)).astype(jnp.bfloat16)
                for k in range(HEADS_AT_ONCE):
                    out_ref[b * BLOCK:(b + 1) * BLOCK, pl.ds(pl.multiple_of((h0 + k) * HD, HD), HD)] = mixed[k]

    for copy in started:
        copy.wait_send()
    for d in range(1, back + 1):
        @pl.when(me_ctx + d < n_ctx)
        def _():
            doc_copy(d).wait_send()
            if d == back:
                for g in range(kv_heads):
                    kv_copy(kv, kv_send, kv_recv, remote, back, span, nb, rows, g, d, me_ctx + d).wait_send()


def kv_copy(kv, send, recv, remote, back, span, nb, rows, g, d, other):
    skip = max(0, d * nb + 1 - span) * BLOCK
    cut = pl.ds(skip, rows - skip)
    return remote(
        kv.at[back, g, cut], kv.at[back - d, g, cut],
        send.at[d - 1, g], recv.at[d - 1, g], {"ctx": other},
    )


def solution(mesh):
    dp, n_ctx, tp = mesh.shape["dp"], mesh.shape["ctx"], mesh.shape["tp"]

    def body(tokens, queries, k_weight, v_weight, doc_blocks):
        rows, width = tokens.shape[1], tokens.shape[2]
        deep, kvw = k_weight.shape
        heads = queries.shape[2] // HD
        nb = rows // BLOCK
        span = nb * n_ctx // 2
        back = -(-(span - 1) // nb)
        groups, pieces = dp // 2, dp // tp
        dma = pltpu.SemaphoreType.DMA
        hbm = pl.BlockSpec(memory_space=pltpu.HBM)
        vmem = pl.BlockSpec(memory_space=pltpu.VMEM)
        out = pl.pallas_call(
            functools.partial(kernel, (dp, n_ctx, tp)),
            out_shape=jax.ShapeDtypeStruct((rows, heads * HD), jnp.bfloat16),
            in_specs=[hbm] * 5,
            out_specs=vmem,
            scratch_shapes=[
                pltpu.VMEM((dp, rows, deep), jnp.bfloat16),
                pltpu.VMEM((rows, heads * HD), jnp.bfloat16),
                pltpu.VMEM((heads, rows, HD), jnp.bfloat16),
                pltpu.VMEM((dp, deep, kvw), jnp.bfloat16),
                pltpu.VMEM((dp, deep, kvw), jnp.bfloat16),
                pltpu.VMEM((rows, 2 * kvw), jnp.float32),
                pltpu.VMEM((back + 1, kvw // HD, rows, 2 * HD), jnp.bfloat16),
                pltpu.VMEM((back + 1, 8, rows), jnp.int32),
                pltpu.VMEM((1, nb), jnp.int32),
                pltpu.VMEM((rows, HD), jnp.float32),
                pltpu.VMEM((rows, HD), jnp.float32),
                dma((4 + pieces,)),
                dma((groups - 1, STEPS, 2)), dma((groups - 1, STEPS, 2)),
                dma((2,)), dma((2,)),
                dma((groups - 1, STEPS, 2)), dma((groups - 1, STEPS, 2)),
                dma((tp - 1, STEPS, pieces)), dma((tp - 1, STEPS, pieces)),
                dma((back, kvw // HD)), dma((back, kvw // HD)),
                dma((back,)), dma((back,)),
            ],
            compiler_params=pltpu.CompilerParams(
                collective_id=0, has_side_effects=True, vmem_limit_bytes=60 << 20
            ),
        )(tokens[0], queries[0], k_weight, v_weight, doc_blocks)
        return out[None]

    placed = (
        P("dp", "ctx", "tp"),
        P("dp", "ctx", "tp"),
        P("dp", "tp"),
        P("dp", "tp"),
        P("dp", "ctx"),
    )
    return jax.shard_map(
        body, mesh=mesh, in_specs=placed, out_specs=P("dp", "ctx", "tp"), check_vma=False
    )
```

```python
import functools
import math

import jax
import jax.numpy as jnp
from jax import lax
from jax.experimental import pallas as pl
from jax.experimental.pallas import tpu as pltpu
from jax.sharding import PartitionSpec as P

HD = 128
BLOCK = 128
STEPS = 4
HEADS_AT_ONCE = 8

ROPE_BASE = 500000.0
YARN_FACTOR = 16.0
PRETRAIN_CONTEXT = 8192.0
BETA_FAST = 32.0
BETA_SLOW = 1.0
ATTN_FACTOR = (1.0 + 0.1 * math.log(16.0)) ** 2
MASKED_SCORE = -1e30
MESH = pl.DeviceIdType.MESH


def yarn_frequency(shape):
    counter = lax.broadcasted_iota(jnp.int32, shape, 1) % (HD // 2)
    base_freq = jnp.exp(counter.astype(jnp.float32) * (-2.0 * math.log(ROPE_BASE) / HD))
    wave_ratio = base_freq * (PRETRAIN_CONTEXT / (2.0 * math.pi))
    ramp = jnp.clip((wave_ratio - BETA_SLOW) / (BETA_FAST - BETA_SLOW), 0.0, 1.0)
    return ramp * base_freq + (1.0 - ramp) * base_freq / YARN_FACTOR


def kernel(
    sizes,
    tok_hbm, q_hbm, kw_hbm, vw_hbm, docs_hbm,
    out_ref,
    tok, qraw, qrot, wk, wv, acc, kv, docs, docs_own, cos_ref, sin_ref,
    loc_sem, y_send, y_recv, s_send, s_recv, f_send, f_recv, z_send, z_recv, t_send, t_recv,
    kv_send, kv_recv, d_send, d_recv,
):
    dp, n_ctx, tp = sizes
    groups = dp // 2
    pieces = dp // tp
    rows = q_hbm.shape[0]
    deep = kw_hbm.shape[0]
    part = deep // STEPS
    kvw = kw_hbm.shape[1]
    kv_heads = kvw // HD
    heads = q_hbm.shape[1] // HD
    back = docs.shape[0] - 1
    nb = rows // BLOCK
    span = nb * n_ctx // 2
    me_dp = lax.axis_index("dp")
    me_ctx = lax.axis_index("ctx")
    me_tp = lax.axis_index("tp")
    group = me_dp // 2
    core = me_dp % 2
    sib = group * 2 + (1 - core)

    def remote(src, dst, send, recv, where):
        return pltpu.make_async_remote_copy(
            src_ref=src, dst_ref=dst, send_sem=send, recv_sem=recv,
            device_id=where, device_id_type=MESH,
        )

    locals_ = [
        pltpu.make_async_copy(q_hbm, qraw, loc_sem.at[0]),
        pltpu.make_async_copy(kw_hbm, wk.at[me_dp], loc_sem.at[1]),
        pltpu.make_async_copy(vw_hbm, wv.at[me_dp], loc_sem.at[2]),
    ]
    for j in range(pieces):
        locals_.append(
            pltpu.make_async_copy(
                tok_hbm.at[:, pl.ds(j * deep, deep)],
                tok.at[me_tp * pieces + j],
                loc_sem.at[3 + j],
            )
        )
    docs_in = pltpu.make_async_copy(docs_hbm, docs_own, loc_sem.at[3 + pieces])
    docs_in.start()
    for one in locals_:
        one.start()

    barrier = pltpu.get_barrier_semaphore()
    fixed = 0
    for r in range(1, groups):
        other = lax.rem(group + r, groups) * 2 + core
        pl.semaphore_signal(barrier, inc=1, device_id={"dp": other}, device_id_type=MESH)
        fixed += 1
    pl.semaphore_signal(barrier, inc=1, device_id={"dp": sib}, device_id_type=MESH)
    fixed += 1
    for r in range(1, tp):
        pl.semaphore_signal(
            barrier, inc=1, device_id={"tp": lax.rem(me_tp + r, tp)}, device_id_type=MESH
        )
        fixed += 1
    for d in range(1, back + 1):
        @pl.when(me_ctx + d < n_ctx)
        def _():
            pl.semaphore_signal(barrier, inc=1, device_id={"ctx": me_ctx + d}, device_id_type=MESH)

        @pl.when(me_ctx - d >= 0)
        def _():
            pl.semaphore_signal(barrier, inc=1, device_id={"ctx": me_ctx - d}, device_id_type=MESH)
    peers = fixed
    for d in range(1, back + 1):
        peers = peers + jnp.where(me_ctx + d < n_ctx, 1, 0) + jnp.where(me_ctx - d >= 0, 1, 0)
    pl.semaphore_wait(barrier, peers)

    started = []
    parity = me_ctx % 2
    pair = me_ctx + 1 - 2 * parity
    half = STEPS // 2
    bufs = ((kw_hbm, wk), (vw_hbm, wv))

    def chunk(k, odd):
        return pl.ds(pl.multiple_of((2 * k + odd) * part, part), part)

    def begin(copy):
        copy.start()
        started.append(copy)

    def y_copy(r, k, w, owner):
        hbm, buf = bufs[w]
        return remote(
            hbm.at[chunk(k, parity)], buf.at[owner, chunk(k, parity)],
            y_send.at[r - 1, k, w], y_recv.at[r - 1, k, w],
            {"dp": lax.rem(group + r, groups) * 2 + core},
        )

    def z_copy(r, k, w, owner, odd):
        buf = bufs[w][1]
        cut = chunk(k, odd)
        return remote(
            buf.at[owner, cut], buf.at[owner, cut],
            z_send.at[r - 1, k, w], z_recv.at[r - 1, k, w], {"ctx": pair},
        )

    def f_copy(r, k, w, owner, odd, slot):
        buf = bufs[w][1]
        cut = chunk(k, odd)
        return remote(
            buf.at[owner, cut], buf.at[owner, cut],
            f_send.at[r - 1, slot, w], f_recv.at[r - 1, slot, w], {"dp": sib},
        )

    def s_copy(w, owner):
        hbm, buf = bufs[w]
        return remote(hbm, buf.at[owner], s_send.at[w], s_recv.at[w], {"dp": sib})

    def t_copy(r, b, j, owner):
        lines = pl.ds(b * BLOCK, BLOCK)
        return remote(
            tok_hbm.at[lines, pl.ds(j * deep, deep)], tok.at[owner * pieces + j, lines, :],
            t_send.at[r - 1, b, j], t_recv.at[r - 1, b, j], {"tp": lax.rem(me_tp + r, tp)},
        )

    def source(r, of_core):
        return lax.rem(group + groups - r, groups) * 2 + of_core

    def start_tokens(b):
        for r in range(1, tp):
            for j in range(pieces):
                begin(t_copy(r, b, j, me_tp))

    for k in range(half):
        for r in range(1, groups):
            for w in range(2):
                begin(y_copy(r, k, w, me_dp))
        if k == 0:
            start_tokens(nb - 1)
            for w in range(2):
                begin(s_copy(w, me_dp))

    def doc_copy(d):
        return remote(
            docs.at[back], docs.at[back - d], d_send.at[d - 1], d_recv.at[d - 1], {"ctx": me_ctx + d}
        )

    def doc_in(d):
        return remote(
            docs.at[back], docs.at[back - d], d_send.at[d - 1], d_recv.at[d - 1], {"ctx": me_ctx - d}
        )

    docs_in.wait()
    lane = lax.broadcasted_iota(jnp.int32, docs.shape[1:], 1)
    spread = jnp.broadcast_to(docs_own[0:1, 0:1], docs.shape[1:])
    for b in range(1, nb):
        spread = jnp.where(lane >= b * BLOCK, docs_own[0:1, b:b + 1], spread)
    docs[back] = spread
    for d in range(1, back + 1):
        @pl.when(me_ctx + d < n_ctx)
        def _():
            doc_copy(d).start()

        @pl.when(me_ctx - d < 0)
        def _():
            docs[back - d] = jnp.full(docs.shape[1:], -1, jnp.int32)
            kv[back - d] = jnp.zeros(kv.shape[1:], kv.dtype)

    position = me_ctx * rows + lax.broadcasted_iota(jnp.int32, (rows, HD), 0)
    angle = position.astype(jnp.float32) * yarn_frequency((1, HD))
    upper = lax.broadcasted_iota(jnp.int32, (rows, HD), 1) >= HD // 2
    cos_ref[...] = jnp.cos(angle)
    sine = jnp.sin(angle)
    sin_ref[...] = jnp.where(upper, sine, -sine)
    for one in locals_:
        one.wait()
    scale = ATTN_FACTOR / math.sqrt(HD)

    @pl.loop(0, heads)
    def _(h):
        u = qraw[:, pl.ds(pl.multiple_of(h * HD, HD), HD)].astype(jnp.float32)
        turned = u * cos_ref[...] + pltpu.roll(u, HD // 2, 1) * sin_ref[...]
        qrot[h] = (turned * scale).astype(jnp.bfloat16)

    acc[...] = jnp.zeros_like(acc)
    for w in range(2):
        s_copy(w, sib).wait_recv()

    for k in range(half):
        for r in range(1, groups):
            for w in range(2):
                y_copy(r, k, w, source(r, core)).wait_recv()
                begin(z_copy(r, k, w, source(r, core), parity))
                begin(f_copy(r, k, w, source(r, core), parity, k))
    for b in reversed(range(nb)):
        for r in range(1, tp):
            if b == nb - 1:
                for j in range(pieces):
                    t_copy(r, b, j, lax.rem(me_tp + tp - r, tp)).wait_recv()
        if b == nb - 1:
            if nb > 1:
                start_tokens(b - 1)
            for k in range(half):
                for r in range(1, groups):
                    for w in range(2):
                        z_copy(r, k, w, source(r, core), 1 - parity).wait_recv()
                        begin(f_copy(r, k, w, source(r, core), 1 - parity, half + k))
            for k in range(half):
                for r in range(1, groups):
                    for w in range(2):
                        f_copy(r, k, w, source(r, 1 - core), parity, k).wait_recv()
                        f_copy(r, k, w, source(r, 1 - core), 1 - parity, half + k).wait_recv()
        lines = slice(b * BLOCK, (b + 1) * BLOCK)

        def add(p):
            x = tok[p, lines, :]
            acc[lines, :kvw] += jnp.dot(x, wk[p], preferred_element_type=jnp.float32)
            acc[lines, kvw:] += jnp.dot(x, wv[p], preferred_element_type=jnp.float32)

        @pl.loop(0, pieces)
        def _(j):
            add(me_tp * pieces + j)

        for r in range(1, tp):
            far = lax.rem(me_tp + tp - r, tp)
            for j in range(pieces):
                if b < nb - 1:
                    t_copy(r, b, j, far).wait_recv()
                add(far * pieces + j)
        if 0 < b < nb - 1:
            start_tokens(b - 1)

        for g in range(kv_heads):
            u = acc[lines, g * HD:(g + 1) * HD]
            turned = u * cos_ref[lines, :] + pltpu.roll(u, HD // 2, 1) * sin_ref[lines, :]
            kv[back, g, lines, :HD] = turned.astype(jnp.bfloat16)
            kv[back, g, lines, HD:] = acc[lines, kvw + g * HD:kvw + (g + 1) * HD].astype(jnp.bfloat16)
        for d in range(1, back + 1):
            if d * nb - b < span:
                @pl.when(me_ctx + d < n_ctx)
                def _():
                    kv_copy(kv, kv_send, kv_recv, remote, back, b, d, me_ctx + d).start()

    for d in range(1, back + 1):
        @pl.when(me_ctx - d >= 0)
        def _():
            doc_in(d).wait_recv()

    wide = span * BLOCK
    keep = []
    for b in range(nb):
        first = back * nb + b + 1 - span
        mine = docs[back, 0:1, b * BLOCK:(b + 1) * BLOCK]
        key_docs = jnp.concatenate(
            [
                docs[(first + k) // nb, 0:1, ((first + k) % nb) * BLOCK:((first + k) % nb + 1) * BLOCK] - mine
                for k in range(span)
            ],
            axis=1,
        )
        column = lax.broadcasted_iota(jnp.int32, (BLOCK, wide), 1) - (span - 1) * BLOCK
        row = lax.broadcasted_iota(jnp.int32, (BLOCK, wide), 0)
        keep.append((column <= row) & (key_docs == 0))

    group_heads = heads // kv_heads
    for d in range(1, back + 1):
        for b in range(nb):
            if d * nb - b < span:
                @pl.when(me_ctx - d >= 0)
                def _():
                    kv_copy(kv, kv_send, kv_recv, remote, back, b, d, me_ctx - d).wait_recv()
    for b in reversed(range(nb)):
        first = back * nb + b + 1 - span
        for g in range(kv_heads):
            window = jnp.concatenate(
                [
                    kv[(first + k) // nb, g, ((first + k) % nb) * BLOCK:((first + k) % nb + 1) * BLOCK, :]
                    for k in range(span)
                ],
                axis=0,
            )
            keys, values = window[:, :HD], window[:, HD:]
            mask = keep[b]

            @pl.loop(0, group_heads // HEADS_AT_ONCE)
            def _(t):
                h0 = g * group_heads + t * HEADS_AT_ONCE
                q = qrot[pl.ds(h0, HEADS_AT_ONCE), b * BLOCK:(b + 1) * BLOCK, :]
                s = lax.dot_general(
                    q.reshape(HEADS_AT_ONCE * BLOCK, HD), keys,
                    (((1,), (1,)), ((), ())), preferred_element_type=jnp.float32,
                ).reshape(HEADS_AT_ONCE, BLOCK, wide)
                s = jnp.where(mask[None], s, MASKED_SCORE)
                top = jnp.max(s, axis=-1, keepdims=True)
                e = jnp.exp(s - top)
                total = jnp.sum(e, axis=-1, keepdims=True)
                mixed = jnp.dot(
                    e.astype(jnp.bfloat16).reshape(HEADS_AT_ONCE * BLOCK, wide), values,
                    preferred_element_type=jnp.float32,
                ).reshape(HEADS_AT_ONCE, BLOCK, HD)
                mixed = (mixed * (1.0 / total)).astype(jnp.bfloat16)
                for k in range(HEADS_AT_ONCE):
                    out_ref[b * BLOCK:(b + 1) * BLOCK, pl.ds(pl.multiple_of((h0 + k) * HD, HD), HD)] = mixed[k]

    for copy in started:
        copy.wait_send()
    for d in range(1, back + 1):
        @pl.when(me_ctx + d < n_ctx)
        def _():
            doc_copy(d).wait_send()
            for b in range(nb):
                if d * nb - b < span:
                    kv_copy(kv, kv_send, kv_recv, remote, back, b, d, me_ctx + d).wait_send()


def kv_copy(kv, send, recv, remote, back, b, d, other):
    lines = pl.ds(b * BLOCK, BLOCK)
    return remote(
        kv.at[back, :, lines], kv.at[back - d, :, lines],
        send.at[d - 1, b], recv.at[d - 1, b], {"ctx": other},
    )


def solution(mesh):
    dp, n_ctx, tp = mesh.shape["dp"], mesh.shape["ctx"], mesh.shape["tp"]

    def body(tokens, queries, k_weight, v_weight, doc_blocks):
        rows, width = tokens.shape[1], tokens.shape[2]
        deep, kvw = k_weight.shape
        heads = queries.shape[2] // HD
        nb = rows // BLOCK
        span = nb * n_ctx // 2
        back = -(-(span - 1) // nb)
        groups, pieces = dp // 2, dp // tp
        dma = pltpu.SemaphoreType.DMA
        hbm = pl.BlockSpec(memory_space=pltpu.HBM)
        vmem = pl.BlockSpec(memory_space=pltpu.VMEM)
        out = pl.pallas_call(
            functools.partial(kernel, (dp, n_ctx, tp)),
            out_shape=jax.ShapeDtypeStruct((rows, heads * HD), jnp.bfloat16),
            in_specs=[hbm] * 5,
            out_specs=vmem,
            scratch_shapes=[
                pltpu.VMEM((dp, rows, deep), jnp.bfloat16),
                pltpu.VMEM((rows, heads * HD), jnp.bfloat16),
                pltpu.VMEM((heads, rows, HD), jnp.bfloat16),
                pltpu.VMEM((dp, deep, kvw), jnp.bfloat16),
                pltpu.VMEM((dp, deep, kvw), jnp.bfloat16),
                pltpu.VMEM((rows, 2 * kvw), jnp.float32),
                pltpu.VMEM((back + 1, kvw // HD, rows, 2 * HD), jnp.bfloat16),
                pltpu.VMEM((back + 1, 8, rows), jnp.int32),
                pltpu.VMEM((1, nb), jnp.int32),
                pltpu.VMEM((rows, HD), jnp.float32),
                pltpu.VMEM((rows, HD), jnp.float32),
                dma((4 + pieces,)),
                dma((groups - 1, STEPS // 2, 2)), dma((groups - 1, STEPS // 2, 2)),
                dma((2,)), dma((2,)),
                dma((groups - 1, STEPS, 2)), dma((groups - 1, STEPS, 2)),
                dma((groups - 1, STEPS // 2, 2)), dma((groups - 1, STEPS // 2, 2)),
                dma((tp - 1, nb, pieces)), dma((tp - 1, nb, pieces)),
                dma((back, nb)), dma((back, nb)),
                dma((back,)), dma((back,)),
            ],
            compiler_params=pltpu.CompilerParams(
                collective_id=0, has_side_effects=True, vmem_limit_bytes=60 << 20
            ),
        )(tokens[0], queries[0], k_weight, v_weight, doc_blocks)
        return out[None]

    placed = (
        P("dp", "ctx", "tp"),
        P("dp", "ctx", "tp"),
        P("dp", "tp"),
        P("dp", "tp"),
        P("dp", "ctx"),
    )
    return jax.shard_map(
        body, mesh=mesh, in_specs=placed, out_specs=P("dp", "ctx", "tp"), check_vma=False
    )
```
